512 devices in a mesh: blk: 16 (over z_hi, x), bulk: 32 (over y, z_lo, core).
Axes of the slice: x: 4, y: 8, z: 8 (z_hi: 4, z_lo: 2; z = z_hi * 2 + z_lo), core: 2. Of those that a mesh axis runs over, the one named last changes fastest.
Arguments:
- currents: bfloat16 [512, 2, 256, 512], P(('blk', 'bulk')), may hold values from -6 to 6
- near_blocks: bfloat16 [512, 2, 2, 512, 512], P(('blk', 'bulk')), may hold values from -0.1875 to 0.1875
- near_list: int32 [512, 1], P(('blk', 'bulk')), may hold values from 0 to 7
- radiate: bfloat16 [512, 2, 512, 384], P(('blk', 'bulk')), may hold values from -0.1875 to 0.1875
- receive: bfloat16 [512, 2, 384, 512], P(('blk', 'bulk')), may hold values from -0.21875 to 0.21875
- far_list: int32 [512, 6], P(('blk', 'bulk')), may hold values from 0 to 511, as said below
- far_count: int32 [512], P(('blk', 'bulk')), may hold values from 3 to 6, as said below
- owner: int32 [512], replicated, may hold values from 0 to 511, as said below
- translation: float32 [512, 6, 2, 384], P(('blk', 'bulk')), may hold values from -3 to 3
Outputs:
- fields: bfloat16 [512, 2, 256, 512], P(('blk', 'bulk'))
The draws below stay inside these ranges and needn't reach their ends.
Inputs may be any that keep to these rules, and one draw needn't show every extreme that they name: A permutation of the box labels that keeps every label in its own slab: owner[L] // 32 == L // 32. `far_list`: each row names 6 distinct labels of boxes held in the row's own slab by devices other than the row's own. `far_count`: the number of leading far_list entries that are used.
All inputs are finite; a program needn't handle non-finite values.
Results may differ from the reference program's by a relative error of at most 0.0051.
Values may be sent and summed in bfloat16 or wider, within the bound.
No kernel may reach another device: no remote copies, remote signals or barrier semaphores. Data moves between devices by JAX's collectives and lax.ppermute only.
A program may use at most 64 MiB of HBM per device.

```python
import jax
import jax.numpy as jnp
from jax import lax

B = 512
P_SIZE = 384
R = 256
FAR = 6
SLABS = 16
ROWBOXES = 32
BOXES = 512


def box_layout(key):
    first, second = jax.random.split(key)
    slab_keys = jax.random.split(first, SLABS)
    places = jax.vmap(lambda k: jax.random.permutation(k, ROWBOXES))(slab_keys).astype(jnp.int32)
    owner = (jnp.arange(SLABS, dtype=jnp.int32)[:, None] * ROWBOXES + places).reshape(BOXES)
    label_of = jnp.argsort(owner, stable=True).astype(jnp.int32)
    scores = jax.random.randint(second, (BOXES, ROWBOXES - 1), 0, 1 << 20)
    scores = scores * ROWBOXES + jnp.arange(ROWBOXES - 1, dtype=jnp.int32)[None, :]
    offsets = jnp.argsort(scores, axis=1, stable=True)[:, :FAR].astype(jnp.int32) + 1
    device = jnp.arange(BOXES, dtype=jnp.int32)[:, None]
    source = device // ROWBOXES * ROWBOXES + (device % ROWBOXES + offsets) % ROWBOXES
    return (owner, label_of[source])


def draw_owner(key, part):
    return box_layout(key)[0]


def draw_far_list(key, part):
    return box_layout(key)[1]


def draw_far_count(key, part):
    key = jax.random.fold_in(key, 3)
    counts = jax.random.randint(key, (BOXES,), FAR // 2, FAR + 1).astype(jnp.int32)
    return counts.at[0].set(FAR)


def set_ends(drawn, own_key, least, largest):
    index_at = [jax.random.randint(jax.random.fold_in(own_key, axis), (), 0, length) for axis, length in enumerate(drawn.shape)]
    main_axis = drawn.shape.index(max(drawn.shape))
    beside = index_at[:main_axis] + [(index_at[main_axis] + 1) % drawn.shape[main_axis]] + index_at[main_axis + 1:]
    return drawn.at[tuple(index_at)].set(least).at[tuple(beside)].set(largest)


def steps_of(key, dims, cuts, least, top_value):
    level, own = 1.0, jax.random.fold_in(key, 6)
    for axis_at, shards_of in cuts:
        heights = jnp.exp(jax.random.uniform(jax.random.fold_in(own, axis_at), (shards_of,), jnp.float32, least / len(cuts), top_value / len(cuts)))
        level = level * jnp.repeat(heights, dims[axis_at] // shards_of).reshape([-1 if axis == axis_at else 1 for axis in range(len(dims))])
    return level


def scatter_about(stream_key, dims, scale, bound, cuts=(), held_as=jnp.bfloat16):
    drawn = scale * jax.random.normal(stream_key, dims, jnp.float32)
    if cuts:
        drawn = drawn * steps_of(stream_key, dims, cuts, -0.22, 0.18)
    return jnp.clip(drawn, -bound, bound).astype(held_as)


def setup_inputs(seed: int = 0) -> dict:
    seeds = jax.random.split(jax.random.key(seed), 10)
    currents = scatter_about(seeds[0], (BOXES, 2, R, B), 1.0, 6.0, ((0, 512),))
    near_blocks = scatter_about(seeds[1], (BOXES, 2, 2, B, B), (2 * B) ** -0.5, 0.1875, ((0, 512),))
    near_list = set_ends(jax.random.randint(seeds[2], (BOXES, 1), 0, 8), jax.random.fold_in(seeds[2], 1), 0, 7).astype(jnp.int32)
    radiate = scatter_about(seeds[3], (BOXES, 2, B, P_SIZE), (2 * B) ** -0.5, 0.1875, ((0, 512),))
    receive = scatter_about(seeds[4], (BOXES, 2, P_SIZE, B), (2 * P_SIZE) ** -0.5, 0.21875, ((0, 512),))
    far_list = draw_far_list(jax.random.fold_in(seeds[9], 71), 0)
    far_count = draw_far_count(jax.random.fold_in(seeds[9], 71), 0)
    owner = draw_owner(jax.random.fold_in(seeds[9], 71), 0)
    translation = scatter_about(seeds[8], (BOXES, FAR, 2, P_SIZE), 0.5, 3.0, ((0, 512),), jnp.float32)
    return {"currents": currents, "near_blocks": near_blocks, "near_list": near_list, "radiate": radiate, "receive": receive, "far_list": far_list, "far_count": far_count, "owner": owner, "translation": translation}


def complex_product(left, right):
    real_part = jnp.dot(left[0], right[0], preferred_element_type=jnp.float32) - jnp.dot(left[1], right[1], preferred_element_type=jnp.float32)
    imag_part = jnp.dot(left[0], right[1], preferred_element_type=jnp.float32) + jnp.dot(left[1], right[0], preferred_element_type=jnp.float32)
    return jnp.stack([real_part, imag_part])


def reference(currents, near_blocks, near_list, radiate, receive, far_list, far_count, owner, translation):
    patterns = lax.map(lambda pair: complex_product(pair[0], pair[1]).astype(jnp.bfloat16), (currents, radiate))
    grid = currents.reshape(SLABS, ROWBOXES, 2, R, B)
    padded = jnp.pad(grid, ((1, 1), (1, 1), (0, 0), (0, 0), (0, 0)))
    slab_step = jnp.array([-1, -1, -1, 0, 0, 1, 1, 1], jnp.int32)
    place_step = jnp.array([-1, 0, 1, -1, 1, -1, 0, 1], jnp.int32)
    sources = owner[far_list]
    used = (jnp.arange(FAR, dtype=jnp.int32)[None, :] < far_count[:, None]).astype(jnp.float32)

    def one_box(index):
        slab = (index // ROWBOXES).astype(jnp.int32)
        place = (index % ROWBOXES).astype(jnp.int32)
        code = near_list[index, 0]
        zero = jnp.zeros((), jnp.int32)
        neighbour = lax.dynamic_slice(padded, (slab + 1 + slab_step[code], place + 1 + place_step[code], zero, zero, zero), (1, 1, 2, R, B))[0, 0]
        blocks = near_blocks[index]
        near = complex_product(currents[index], blocks[0]) + complex_product(neighbour, blocks[1])
        chosen = patterns[sources[index]].astype(jnp.float32)
        factors = translation[index] * used[index][:, None, None]
        fr = factors[:, 0][:, None, :]
        fi = factors[:, 1][:, None, :]
        incoming_re = jnp.sum(fr * chosen[:, 0] - fi * chosen[:, 1], axis=0)
        incoming_im = jnp.sum(fr * chosen[:, 1] + fi * chosen[:, 0], axis=0)
        incoming = jnp.stack([incoming_re, incoming_im]).astype(jnp.bfloat16)
        far = complex_product(incoming, receive[index])
        return (near + far).astype(jnp.bfloat16)

    return lax.map(one_box, jnp.arange(BOXES, dtype=jnp.int32))
```

```python
import jax
import jax.numpy as jnp
from jax import lax
from jax.experimental import pallas as pl
from jax.experimental.pallas import tpu as pltpu
from jax.sharding import PartitionSpec as P

F32, BF16, I32 = jnp.float32, jnp.bfloat16, jnp.int32
VMEM = pl.BlockSpec(memory_space=pltpu.VMEM)
SMEM = pl.BlockSpec(memory_space=pltpu.SMEM)
ANY = pl.BlockSpec(memory_space=pl.ANY)
LOW, MIXED, SOURCE, CODE = 16, 32, 64, 72


def dot(left, right):
    return jnp.dot(left, right, preferred_element_type=F32)


def product(left_re, left_im, right):
    return (
        dot(left_re, right[0]) - dot(left_im, right[1]),
        dot(left_re, right[1]) + dot(left_im, right[0]),
    )


def params(flops, moved):
    return dict(
        compiler_params=pltpu.CompilerParams(vmem_limit_bytes=40 << 20),
        cost_estimate=pl.CostEstimate(flops=flops, bytes_accessed=moved, transcendentals=0),
    )


def split_rows(first, second):
    top = lax.broadcasted_iota(I32, first.shape, 0) < 4
    return (
        jnp.where(top, first, pltpu.roll(second, 4, 0)),
        jnp.where(top, pltpu.roll(first, 4, 0), second),
    )


def radiate_kernel(far_list, far_count, owner, near_list, currents, radiate, translation, out, table):
    group, _, width = out.shape
    real, imag = product(currents[0], currents[1], radiate)
    waves = real.shape[0]
    table[...] = jnp.zeros_like(table)
    angles = table.shape[1]
    for k in range(translation.shape[0]):
        factor = jnp.where(k < far_count[0], translation[k], 0.0)
        high = factor.astype(BF16).astype(F32)
        for base in (0, MIXED):
            table[base + 2 * k : base + 2 * k + 2, :] = high
            table[base + LOW + 2 * k : base + LOW + 2 * k + 2, :] = factor - high
        source = lax.rem(owner[far_list[0, k]], group).astype(F32)
        table[SOURCE + k : SOURCE + k + 1, :] = jnp.full((1, angles), source, F32)
    table[CODE : CODE + 1, :] = jnp.full((1, angles), near_list[0, 0].astype(F32), F32)
    tiles = angles // 8
    real = real.T.reshape(tiles, 8, waves)
    imag = imag.T.reshape(tiles, 8, waves)
    factors = table[...].T.reshape(tiles, 8, table.shape[0])
    lane = lax.broadcasted_iota(I32, factors.shape[1:], 1)
    in_mixed = (lane >= MIXED) & (lane < SOURCE)
    for pair in range(group // 2):
        a, b, c = 3 * pair, 3 * pair + 1, 3 * pair + 2
        mixed = split_rows(real[b], imag[b])
        mixed_factors = split_rows(factors[b], factors[b])
        for side, tile in ((0, a), (1, c)):
            beside = jnp.where(in_mixed, mixed_factors[side], factors[tile])
            whole = jnp.concatenate([real[tile], imag[tile], mixed[side], beside], axis=1)
            out[2 * pair + side] = whole.astype(BF16)


def translate_kernel(chunks, out, codes, values, turned, numbers, table, sem):
    group, _, width = out.shape
    waves = width // 3
    for t in range(group):
        values[t] = chunks[t, :, :width].astype(F32)
        turned[t] = pltpu.roll(values[t, :, 2 * waves :], 4, 0)
        numbers[t : t + 1, :] = chunks[t, :, width:].astype(F32)[0:1, :].astype(I32)
    codes[...] = numbers[...]
    copy = pltpu.make_async_copy(numbers, table, sem)
    copy.start()
    copy.wait()
    sign = jnp.where(lax.broadcasted_iota(I32, (8, 1), 0) < 4, -1.0, 1.0)

    def target(t, carry):
        split = chunks[t, :, width:].astype(F32)
        factor = split + pltpu.roll(split, 128 - LOW, 1)
        real = jnp.zeros((8, waves), F32)
        imag, mixed = real, real
        for k in range(6):
            source = table[t, SOURCE + k]
            fr, fi = factor[:, 2 * k : 2 * k + 1], factor[:, 2 * k + 1 : 2 * k + 2]
            mr = factor[:, MIXED + 2 * k : MIXED + 2 * k + 1]
            mi = factor[:, MIXED + 2 * k + 1 : MIXED + 2 * k + 2] * sign
            re, im = values[source, :, :waves], values[source, :, waves : 2 * waves]
            real += fr * re - fi * im
            imag += fr * im + fi * re
            mixed += mr * values[source, :, 2 * waves :] + mi * turned[source]
        out[t] = jnp.concatenate([real, imag, mixed], axis=1).astype(BF16)
        return carry

    lax.fori_loop(0, group, target, 0)


def select_kernel(place, codes, currents, across, beyond, to_sibling, to_other, sems):
    slab, spot = place[0], place[1]
    even = lax.rem(slab, 2) == 0
    group = codes.shape[0]
    sibling = jnp.where(lax.rem(spot, 2) == 0, spot + 1, spot - 1)
    other = jnp.where(lax.rem(spot, 2) == 0, spot - 1, spot + 1)
    other = jnp.clip(other, 0, group - 1)
    for n, (partner, out) in enumerate(((sibling, to_sibling), (other, to_other))):
        code = codes[partner, CODE]
        same = (code == 3) | (code == 4)
        use_across = (code > 4) == even

        @pl.when(same)
        def _(out=out, n=n):
            pltpu.make_async_copy(currents, out, sems.at[n]).start()

        @pl.when(jnp.logical_not(same) & use_across)
        def _(out=out, n=n):
            pltpu.make_async_copy(across, out, sems.at[n]).start()

        @pl.when(jnp.logical_not(same) & jnp.logical_not(use_across))
        def _(out=out, n=n):
            pltpu.make_async_copy(beyond, out, sems.at[n]).start()

    for n, out in enumerate((to_sibling, to_other)):
        pltpu.make_async_copy(currents, out, sems.at[n]).wait()


def own_kernel(currents, blocks, out):
    real, imag = product(currents[0], currents[1], blocks)
    out[0] = real
    out[1] = imag


def near_kernel(place, near_list, own, across, beyond, sibling, other, blocks, out, chosen, sem):
    slab, spot = place[0], place[1]
    code = near_list[0, 0]
    slab_even, spot_even = lax.rem(slab, 2) == 0, lax.rem(spot, 2) == 0
    straight = (code == 1) | (code == 6)
    use_across = (code > 4) == slab_even
    onward = (code == 2) | (code == 4) | (code == 7)
    use_sibling = onward == spot_even
    for source, wanted in (
        (across, straight & use_across),
        (beyond, straight & jnp.logical_not(use_across)),
        (sibling, jnp.logical_not(straight) & use_sibling),
        (other, jnp.logical_not(straight) & jnp.logical_not(use_sibling)),
    ):

        @pl.when(wanted)
        def _(source=source):
            pltpu.make_async_copy(source, chosen, sem).start()

    pltpu.make_async_copy(across, chosen, sem).wait()
    real, imag = product(chosen[0], chosen[1], blocks)
    out[0] = own[0] + real
    out[1] = own[1] + imag


def receive_kernel(incoming, receive, near, out):
    group, _, width = incoming.shape
    waves = width // 3
    reals, imags = [], []
    for pair in range(group // 2):
        first = incoming[2 * pair].astype(F32)
        second = incoming[2 * pair + 1].astype(F32)
        mixed = split_rows(first[:, 2 * waves :], second[:, 2 * waves :])
        reals += [first[:, :waves], mixed[0], second[:, :waves]]
        imags += [first[:, waves : 2 * waves], mixed[1], second[:, waves : 2 * waves]]
    left_re = jnp.concatenate(reals, axis=0).T.astype(BF16)
    left_im = jnp.concatenate(imags, axis=0).T.astype(BF16)
    real, imag = product(left_re, left_im, receive)
    out[0] = (near[0] + real).astype(BF16)
    out[1] = (near[1] + imag).astype(BF16)


def per_device(
    currents, near_blocks, near_list, radiate, receive, far_list, far_count, owner, translation
):
    local = currents[0]
    _, waves, unknowns = local.shape
    angles = radiate.shape[-1]
    slabs, group = lax.axis_size("blk"), lax.axis_size("bulk")
    place = jnp.stack([lax.axis_index("blk"), lax.axis_index("bulk")]).astype(I32)
    inner = [(i, i ^ 1) for i in range(slabs)]
    outer = [(i, j) for m in range(1, slabs - 1, 2) for i, j in ((m, m + 1), (m + 1, m))]
    side_inner = [(i, i ^ 1) for i in range(group)]
    side_outer = [(i, j) for m in range(1, group - 1, 2) for i, j in ((m, m + 1), (m + 1, m))]
    beyond = lax.ppermute(local, "blk", outer)
    chunk = 3 * waves
    payload = pl.pallas_call(
        radiate_kernel,
        out_shape=jax.ShapeDtypeStruct((group, 8, chunk + 128), BF16),
        in_specs=[SMEM] * 4 + [VMEM] * 3,
        out_specs=VMEM,
        scratch_shapes=[pltpu.VMEM((128, angles), F32)],
        name="radiate",
        **params(8 * waves * unknowns * angles, 2 << 20),
    )(far_list, far_count, owner, near_list, local, radiate[0], translation[0])
    spread = lax.all_to_all(payload, "bulk", 0, 0, tiled=True)
    across = lax.ppermute(local, "blk", inner)
    own = pl.pallas_call(
        own_kernel,
        out_shape=jax.ShapeDtypeStruct((2, waves, unknowns), F32),
        in_specs=[VMEM] * 2,
        out_specs=VMEM,
        name="near_own",
        **params(8 * waves * unknowns * unknowns, 3 << 20),
    )(local, near_blocks[0, 0])
    translated, codes = pl.pallas_call(
        translate_kernel,
        out_shape=(
            jax.ShapeDtypeStruct((group, 8, chunk), BF16),
            jax.ShapeDtypeStruct((group, 128), I32),
        ),
        in_specs=[VMEM],
        out_specs=(VMEM, VMEM),
        scratch_shapes=[
            pltpu.VMEM((group, 8, chunk), F32),
            pltpu.VMEM((group, 8, waves), F32),
            pltpu.VMEM((group, 128), I32),
            pltpu.SMEM((group, 128), I32),
            pltpu.SemaphoreType.DMA,
        ],
        name="translate",
        **params(40 << 20, 1 << 20),
    )(spread)
    incoming = lax.all_to_all(translated, "bulk", 0, 0, tiled=True)
    to_sibling, to_other = pl.pallas_call(
        select_kernel,
        out_shape=(jax.ShapeDtypeStruct(local.shape, BF16),) * 2,
        in_specs=[SMEM] * 2 + [ANY] * 3,
        out_specs=(ANY, ANY),
        scratch_shapes=[pltpu.SemaphoreType.DMA((2,))],
        name="select",
        **params(0, 2 << 20),
    )(place, codes, local, across, beyond)
    sibling = lax.ppermute(to_sibling, "bulk", side_inner)
    other = lax.ppermute(to_other, "bulk", side_outer)
    near = pl.pallas_call(
        near_kernel,
        out_shape=jax.ShapeDtypeStruct((2, waves, unknowns), F32),
        in_specs=[SMEM] * 2 + [VMEM] + [ANY] * 4 + [VMEM],
        out_specs=VMEM,
        scratch_shapes=[pltpu.VMEM(local.shape, BF16), pltpu.SemaphoreType.DMA],
        name="near_beside",
        **params(8 * waves * unknowns * unknowns, 3 << 20),
    )(place, near_list, own, across, beyond, sibling, other, near_blocks[0, 1])
    fields = pl.pallas_call(
        receive_kernel,
        out_shape=jax.ShapeDtypeStruct(local.shape, BF16),
        in_specs=[VMEM] * 3,
        out_specs=VMEM,
        name="receive",
        **params(8 * waves * unknowns * angles, 3 << 20),
    )(incoming, receive[0], near)
    return fields[None]


def solution(mesh):
    boxes = ("blk", "bulk")
    return jax.shard_map(
        per_device,
        mesh=mesh,
        in_specs=(
            P(boxes, None, None, None),
            P(boxes, None, None, None, None),
            P(boxes, None),
            P(boxes, None, None, None),
            P(boxes, None, None, None),
            P(boxes, None),
            P(boxes),
            P(),
            P(boxes, None, None, None),
        ),
        out_specs=P(boxes, None, None, None),
        check_vma=False,
    )
```

```python
import jax
import jax.numpy as jnp
from jax import lax
from jax.experimental import pallas as pl
from jax.experimental.pallas import tpu as pltpu
from jax.sharding import PartitionSpec as P

F32, BF16, I32 = jnp.float32, jnp.bfloat16, jnp.int32
VMEM = pl.BlockSpec(memory_space=pltpu.VMEM)
SMEM = pl.BlockSpec(memory_space=pltpu.SMEM)
ANY = pl.BlockSpec(memory_space=pl.ANY)
HBM = pl.BlockSpec(memory_space=pltpu.HBM)
LOW, MIXED, SOURCE, CODE = 16, 32, 64, 72


def dot(left, right):
    return jnp.dot(left, right, preferred_element_type=F32)


def product(left_re, left_im, right):
    return (
        dot(left_re, right[0]) - dot(left_im, right[1]),
        dot(left_re, right[1]) + dot(left_im, right[0]),
    )


def params(flops, moved, limit=40 << 20):
    return dict(
        compiler_params=pltpu.CompilerParams(vmem_limit_bytes=limit),
        cost_estimate=pl.CostEstimate(flops=flops, bytes_accessed=moved, transcendentals=0),
    )


def split_rows(first, second):
    top = lax.broadcasted_iota(I32, first.shape, 0) < 4
    return (
        jnp.where(top, first, pltpu.roll(second, 4, 0)),
        jnp.where(top, pltpu.roll(first, 4, 0), second),
    )


def radiate_kernel(
    far_list_at, far_count_at, near_list_at, owner_at, currents_at, radiate_at, translation_at, out_at,
    far_list, far_count, near_list, owner, currents, radiate, translation, table, out, sems, out_sems,
):
    small = (
        (far_list_at, far_list),
        (far_count_at, far_count),
        (near_list_at, near_list),
        (owner_at, owner),
        (translation_at, translation),
    )
    large = [(currents_at.at[p], currents.at[p]) for p in range(2)]
    large += [(radiate_at.at[p], radiate.at[p]) for p in range(2)]
    copies = [
        pltpu.make_async_copy(source, target, sems.at[n])
        for n, (source, target) in enumerate((*small, *large))
    ]
    for copy in copies:
        copy.start()
    group, _, width = out.shape
    angles = table.shape[1]
    far = translation.shape[0]
    table[...] = jnp.zeros_like(table)
    for copy in copies[: len(small)]:
        copy.wait()
    for k in range(far):
        factor = jnp.where(k < far_count[0], translation[k], 0.0)
        high = factor.astype(BF16).astype(F32)
        for base in (0, MIXED):
            table[base + 2 * k : base + 2 * k + 2, :] = high
            table[base + LOW + 2 * k : base + LOW + 2 * k + 2, :] = factor - high
        source = lax.rem(owner[far_list[0, k]], group).astype(F32)
        table[SOURCE + k : SOURCE + k + 1, :] = jnp.full((1, angles), source, F32)
    table[CODE : CODE + 1, :] = jnp.full((1, angles), near_list[0, 0].astype(F32), F32)
    for copy in copies[len(small) :]:
        copy.wait()
    waves = currents.shape[1]

    def turned(part, side):
        return lax.dot_general(radiate[part], currents[side], (((0,), (1,)), ((), ())), preferred_element_type=F32)

    real = turned(0, 0) - turned(1, 1)
    imag = turned(1, 0) + turned(0, 1)
    tiles = angles // 8
    real = real.reshape(tiles, 8, waves)
    imag = imag.reshape(tiles, 8, waves)
    factors = table[...].T.reshape(tiles, 8, table.shape[0])
    lane = lax.broadcasted_iota(I32, factors.shape[1:], 1)
    in_mixed = (lane >= MIXED) & (lane < SOURCE)
    def result(step):
        part = pl.ds(group // 4 * step, group // 4)
        return pltpu.make_async_copy(out.at[part], out_at.at[part], out_sems.at[step])

    for pair in range(group // 2):
        a, b, c = 3 * pair, 3 * pair + 1, 3 * pair + 2
        mixed = split_rows(real[b], imag[b])
        mixed_factors = split_rows(factors[b], factors[b])
        for side, tile in ((0, a), (1, c)):
            beside = jnp.where(in_mixed, mixed_factors[side], factors[tile])
            whole = jnp.concatenate([real[tile], imag[tile], mixed[side], beside], axis=1)
            out[2 * pair + side] = whole.astype(BF16)
        if pair % (group // 8) == group // 8 - 1:
            result(pair // (group // 8)).start()
    for step in range(4):
        result(step).wait()


def translate_kernel(chunks, out_at, codes, out, values, turned, numbers, table, sem, sems):
    group, _, width = out.shape
    waves = width // 3
    numbers[...] = chunks[:, :, width:].astype(F32)[:, 0, :].astype(I32)
    copy = pltpu.make_async_copy(numbers, table, sem)
    copy.start()
    for t in range(group):
        values[t] = chunks[t, :, :width].astype(F32)
        turned[t] = pltpu.roll(values[t, :, 2 * waves :], 4, 0)
    codes[...] = numbers[...]
    copy.wait()
    sign = jnp.where(lax.broadcasted_iota(I32, (8, 128), 0) < 4, -1.0, 1.0)

    def target(t):
        split = chunks[t, :, width:].astype(F32)
        factor = split + pltpu.roll(split, 128 - LOW, 1)
        signed = factor * sign
        real = jnp.zeros((8, waves), F32)
        imag, mixed = real, real
        for k in range(6):
            source = table[t, SOURCE + k]
            fr, fi = factor[:, 2 * k : 2 * k + 1], factor[:, 2 * k + 1 : 2 * k + 2]
            mr = factor[:, MIXED + 2 * k : MIXED + 2 * k + 1]
            mi = signed[:, MIXED + 2 * k + 1 : MIXED + 2 * k + 2]
            re, im = values[source, :, :waves], values[source, :, waves : 2 * waves]
            real += fr * re - fi * im
            imag += fr * im + fi * re
            mixed += mr * values[source, :, 2 * waves :] + mi * turned[source]
        out[t] = jnp.concatenate([real, imag, mixed], axis=1).astype(BF16)

    def result(step):
        part = pl.ds(8 * step, 8)
        return pltpu.make_async_copy(out.at[part], out_at.at[part], sems.at[step])

    for step in range(group // 8):
        for t in range(8):
            target(8 * step + t)
        result(step).start()
    for step in range(group // 8):
        result(step).wait()


def gate_kernel(arrived, out):
    out[0] = 0


def gate(arrived, cost):
    token = pl.pallas_call(
        gate_kernel,
        out_shape=jax.ShapeDtypeStruct((1,), I32),
        in_specs=[ANY],
        out_specs=SMEM,
        name="gate",
        **params(cost, 0),
    )(arrived)
    return lax.optimization_barrier((arrived, token))[0]


def came_relayed(place):
    end = lax.rem(place[0], 4)
    return ((end == 0) | (end == 3)) & (lax.rem(place[1], 2) == 1)


def pieces(source, target, sems):
    half = source.shape[1] // 2
    return [
        pltpu.make_async_copy(
            source.at[part, pl.ds(row, half)], target.at[part, pl.ds(row, half)], sems.at[2 * part + row // half]
        )
        for part in range(2)
        for row in (0, half)
    ]


def select_kernel(place, codes, currents, across, beyond, relayed, to_other, to_sibling, sems):
    spot = place[1]
    turned = came_relayed(place)
    for n, (step, out) in enumerate(((-1, to_other), (1, to_sibling))):
        partner = jnp.where(lax.rem(spot, 2) == 0, spot + step, spot - step)
        code = codes[jnp.clip(partner, 0, codes.shape[0] - 1), CODE]
        same = (code == 3) | (code == 4)
        use_across = (code > 4) == (lax.rem(place[0], 2) == 0)
        for source, wanted in (
            (currents, same),
            (across, jnp.logical_not(same) & use_across),
            (beyond, jnp.logical_not(same | use_across | turned)),
            (relayed, jnp.logical_not(same | use_across) & turned),
        ):

            @pl.when(wanted)
            def _(source=source, out=out, n=n):
                for copy in pieces(source, out, sems.at[n]):
                    copy.start()

    for n, out in enumerate((to_other, to_sibling)):
        for copy in pieces(currents, out, sems.at[n]):
            copy.wait()


def receive_kernel(incoming, receive, currents, blocks, out):
    group, _, width = incoming.shape
    waves = width // 3
    reals, imags = [], []
    for pair in range(group // 2):
        first = incoming[2 * pair].astype(F32)
        second = incoming[2 * pair + 1].astype(F32)
        mixed = split_rows(first[:, 2 * waves :], second[:, 2 * waves :])
        reals += [first[:, :waves], mixed[0], second[:, :waves]]
        imags += [first[:, waves : 2 * waves], mixed[1], second[:, waves : 2 * waves]]
    left_re = jnp.concatenate(reals, axis=0).T.astype(BF16)
    left_im = jnp.concatenate(imags, axis=0).T.astype(BF16)
    real, imag = product(left_re, left_im, receive)
    own_re, own_im = product(currents[0], currents[1], blocks.at[0, 0])
    out[0] = own_re + real
    out[1] = own_im + imag


def near_kernel(place, near_list, partial, across, beyond, relayed, other, sibling, blocks, out_at, chosen, out, sems, out_sems):
    code = near_list[0, 0]
    straight = (code == 1) | (code == 6)
    use_across = (code > 4) == (lax.rem(place[0], 2) == 0)
    onward = (code == 2) | (code == 4) | (code == 7)
    turned = came_relayed(place)
    use_sibling = onward == (lax.rem(place[1], 2) == 0)
    for source, wanted in (
        (across, straight & use_across),
        (beyond, straight & jnp.logical_not(use_across | turned)),
        (relayed, straight & jnp.logical_not(use_across) & turned),
        (sibling, jnp.logical_not(straight) & use_sibling),
        (other, jnp.logical_not(straight) & jnp.logical_not(use_sibling)),
    ):

        @pl.when(wanted)
        def _(source=source):
            for copy in pieces(source, chosen, sems):
                copy.start()

    waits = pieces(across, chosen, sems)
    half = chosen.shape[1] // 2

    def result(part, step):
        rows = pl.ds(step * half, half)
        return pltpu.make_async_copy(out.at[part, rows], out_at.at[0, part, rows], out_sems.at[2 * part + step])

    for step in range(2):
        rows = pl.ds(step * half, half)
        for part in range(2):
            waits[2 * part + step].wait()
        real, imag = product(chosen[0, rows], chosen[1, rows], blocks.at[0, 1])
        for part, value in enumerate((real, imag)):
            out[part, rows] = (partial[part, rows] + value).astype(BF16)
            result(part, step).start()
    for step in range(2):
        for part in range(2):
            result(part, step).wait()


def per_device(
    currents, near_blocks, near_list, radiate, receive, far_list, far_count, owner, translation
):
    local = currents[0]
    _, waves, unknowns = local.shape
    angles = radiate.shape[-1]
    slabs, group = lax.axis_size("blk"), lax.axis_size("bulk")
    row = 4
    place = jnp.stack([lax.axis_index("blk"), lax.axis_index("bulk")]).astype(I32)
    inner = [(i, i ^ 1) for i in range(slabs)]
    outer = [(i, j) for m in range(1, slabs - 1, 2) for i, j in ((m, m + 1), (m + 1, m))]
    side_inner = [(i, i ^ 1) for i in range(group)]
    side_outer = [(i, j) for m in range(1, group - 1, 2) for i, j in ((m, m + 1), (m + 1, m))]
    chunk = 3 * waves
    payload = pl.pallas_call(
        radiate_kernel,
        out_shape=jax.ShapeDtypeStruct((group, 8, chunk + 128), BF16),
        in_specs=[ANY] * 7,
        out_specs=HBM,
        scratch_shapes=[
            pltpu.SMEM(far_list.shape, I32),
            pltpu.SMEM(far_count.shape, I32),
            pltpu.SMEM(near_list.shape, I32),
            pltpu.SMEM(owner.shape, I32),
            pltpu.VMEM(local.shape, BF16),
            pltpu.VMEM(radiate.shape[1:], BF16),
            pltpu.VMEM(translation.shape[1:], F32),
            pltpu.VMEM((128, angles), F32),
            pltpu.VMEM((group, 8, chunk + 128), BF16),
            pltpu.SemaphoreType.DMA((9,)),
            pltpu.SemaphoreType.DMA((4,)),
        ],
        name="radiate",
        **params(8 * waves * unknowns * angles, 2 << 20, 60 << 20),
    )(far_list, far_count, near_list, owner, local, radiate[0], translation[0])
    spread = lax.all_to_all(payload, "bulk", 0, 0, tiled=True)
    axes = ("blk", "bulk")
    direct, aside, onward = [], [], []
    for i, j in outer:
        for spot in range(group):
            if min(i, j) % row == row - 1 and spot % 2:
                turn = i - i % row if i < j else i + row - 1
                aside.append((i * group + spot, turn * group + spot))
                onward.append((turn * group + spot, j * group + spot))
            else:
                direct.append((i * group + spot, j * group + spot))
    relayed = gate(lax.ppermute(local, axes, aside), 8_000_000_000)
    beyond = lax.ppermute(local, axes, direct), lax.ppermute(relayed, axes, onward)
    across = lax.ppermute(local, "blk", inner)
    translated, codes = pl.pallas_call(
        translate_kernel,
        out_shape=(
            jax.ShapeDtypeStruct((group, 8, chunk), BF16),
            jax.ShapeDtypeStruct((group, 128), I32),
        ),
        in_specs=[VMEM],
        out_specs=(HBM, VMEM),
        scratch_shapes=[
            pltpu.VMEM((group, 8, chunk), BF16),
            pltpu.VMEM((group, 8, chunk), F32),
            pltpu.VMEM((group, 8, waves), F32),
            pltpu.VMEM((group, 128), I32),
            pltpu.SMEM((group, 128), I32),
            pltpu.SemaphoreType.DMA,
            pltpu.SemaphoreType.DMA((group // 8,)),
        ],
        name="translate",
        **params(0, 4 << 20),
    )(spread)
    incoming = lax.all_to_all(translated, "bulk", 0, 0, tiled=True)
    to_other, to_sibling = pl.pallas_call(
        select_kernel,
        out_shape=(jax.ShapeDtypeStruct(local.shape, BF16),) * 2,
        in_specs=[SMEM] * 2 + [ANY] * 4,
        out_specs=(VMEM, VMEM),
        scratch_shapes=[pltpu.SemaphoreType.DMA((2, 4))],
        name="select",
        **params(0, 2 << 20),
    )(place, codes, local, across, *beyond)
    other = lax.ppermute(to_other, "bulk", side_outer)
    sibling = lax.ppermute(to_sibling, "bulk", side_inner)
    partial = pl.pallas_call(
        receive_kernel,
        out_shape=jax.ShapeDtypeStruct((2, waves, unknowns), F32),
        in_specs=[VMEM] * 4,
        out_specs=VMEM,
        name="receive",
        **params(8 * waves * unknowns * angles, 3 << 20),
    )(incoming, receive[0], local, near_blocks)
    return pl.pallas_call(
        near_kernel,
        out_shape=jax.ShapeDtypeStruct((1, *local.shape), BF16),
        in_specs=[SMEM] * 2 + [VMEM] + [ANY] * 5 + [VMEM],
        out_specs=HBM,
        scratch_shapes=[
            pltpu.VMEM(local.shape, BF16),
            pltpu.VMEM(local.shape, BF16),
            pltpu.SemaphoreType.DMA((4,)),
            pltpu.SemaphoreType.DMA((4,)),
        ],
        name="near",
        **params(8 * waves * unknowns * unknowns, 5 << 20),
    )(place, near_list, partial, across, *beyond, other, sibling, near_blocks)


def solution(mesh):
    boxes = ("blk", "bulk")
    return jax.shard_map(
        per_device,
        mesh=mesh,
        in_specs=(
            P(boxes, None, None, None),
            P(boxes, None, None, None, None),
            P(boxes, None),
            P(boxes, None, None, None),
            P(boxes, None, None, None),
            P(boxes, None),
            P(boxes),
            P(),
            P(boxes, None, None, None),
        ),
        out_specs=P(boxes, None, None, None),
        check_vma=False,
    )
```

```python
import jax
import jax.numpy as jnp
from jax import lax
from jax.experimental import pallas as pl
from jax.experimental.pallas import tpu as pltpu
from jax.sharding import PartitionSpec as P

F32, BF16, I32 = jnp.float32, jnp.bfloat16, jnp.int32
VMEM = pl.BlockSpec(memory_space=pltpu.VMEM)
SMEM = pl.BlockSpec(memory_space=pltpu.SMEM)
ANY = pl.BlockSpec(memory_space=pl.ANY)
HBM = pl.BlockSpec(memory_space=pltpu.HBM)
LOW, MIXED, SOURCE, CODE = 16, 32, 64, 72


def dot(left, right):
    return jnp.dot(left, right, preferred_element_type=F32)


def product(left_re, left_im, right):
    return (
        dot(left_re, right[0]) - dot(left_im, right[1]),
        dot(left_re, right[1]) + dot(left_im, right[0]),
    )


def params(flops, moved, limit=40 << 20):
    return dict(
        compiler_params=pltpu.CompilerParams(vmem_limit_bytes=limit),
        cost_estimate=pl.CostEstimate(flops=flops, bytes_accessed=moved, transcendentals=0),
    )


def split_rows(first, second):
    top = lax.broadcasted_iota(I32, first.shape, 0) < 4
    return (
        jnp.where(top, first, pltpu.roll(second, 4, 0)),
        jnp.where(top, pltpu.roll(first, 4, 0), second),
    )


def radiate_kernel(
    far_list_at, far_count_at, near_list_at, owner_at, currents_at, radiate_at, translation_at, out_at,
    far_list, far_count, near_list, owner, currents, radiate, translation, table, out, sems, out_sems,
):
    small = (
        (far_list_at, far_list),
        (far_count_at, far_count),
        (near_list_at, near_list),
        (owner_at, owner),
        (translation_at, translation),
    )
    large = [(currents_at.at[p], currents.at[p]) for p in range(2)]
    large += [(radiate_at.at[p], radiate.at[p]) for p in range(2)]
    copies = [
        pltpu.make_async_copy(source, target, sems.at[n])
        for n, (source, target) in enumerate((*small, *large))
    ]
    for copy in copies:
        copy.start()
    group, _, width = out.shape
    angles = table.shape[1]
    far = translation.shape[0]
    table[...] = jnp.zeros_like(table)
    for copy in copies[: len(small)]:
        copy.wait()
    for k in range(far):
        factor = jnp.where(k < far_count[0], translation[k], 0.0)
        high = factor.astype(BF16).astype(F32)
        for base in (0, MIXED):
            table[base + 2 * k : base + 2 * k + 2, :] = high
            table[base + LOW + 2 * k : base + LOW + 2 * k + 2, :] = factor - high
        source = lax.rem(owner[far_list[0, k]], group).astype(F32)
        table[SOURCE + k : SOURCE + k + 1, :] = jnp.full((1, angles), source, F32)
    table[CODE : CODE + 1, :] = jnp.full((1, angles), near_list[0, 0].astype(F32), F32)
    for copy in copies[len(small) :]:
        copy.wait()
    waves = currents.shape[1]

    def turned(part, side):
        return lax.dot_general(radiate[part], currents[side], (((0,), (1,)), ((), ())), preferred_element_type=F32)

    real = turned(0, 0) - turned(1, 1)
    imag = turned(1, 0) + turned(0, 1)
    tiles = angles // 8
    real = real.reshape(tiles, 8, waves)
    imag = imag.reshape(tiles, 8, waves)
    factors = table[...].T.reshape(tiles, 8, table.shape[0])
    lane = lax.broadcasted_iota(I32, factors.shape[1:], 1)
    in_mixed = (lane >= MIXED) & (lane < SOURCE)
    def result(step):
        part = pl.ds(group // 4 * step, group // 4)
        return pltpu.make_async_copy(out.at[part], out_at.at[part], out_sems.at[step])

    for pair in range(group // 2):
        a, b, c = 3 * pair, 3 * pair + 1, 3 * pair + 2
        mixed = split_rows(real[b], imag[b])
        mixed_factors = split_rows(factors[b], factors[b])
        for side, tile in ((0, a), (1, c)):
            beside = jnp.where(in_mixed, mixed_factors[side], factors[tile])
            whole = jnp.concatenate([real[tile], imag[tile], mixed[side], beside], axis=1)
            out[2 * pair + side] = whole.astype(BF16)
        if pair % (group // 8) == group // 8 - 1:
            result(pair // (group // 8)).start()
    for step in range(4):
        result(step).wait()


def translate_kernel(chunks, out_at, codes, out, values, turned, numbers, table, sem, sems):
    group, _, width = out.shape
    waves = width // 3
    numbers[...] = chunks[:, :, width:].astype(F32)[:, 0, :].astype(I32)
    copy = pltpu.make_async_copy(numbers, table, sem)
    copy.start()
    for t in range(group):
        values[t] = chunks[t, :, :width].astype(F32)
        turned[t] = pltpu.roll(values[t, :, 2 * waves :], 4, 0)
    codes[...] = numbers[...]
    copy.wait()
    sign = jnp.where(lax.broadcasted_iota(I32, (8, 128), 0) < 4, -1.0, 1.0)

    def target(t):
        split = chunks[t, :, width:].astype(F32)
        factor = split + pltpu.roll(split, 128 - LOW, 1)
        signed = factor * sign
        real = jnp.zeros((8, waves), F32)
        imag, mixed = real, real
        for k in range(6):
            source = table[t, SOURCE + k]
            fr, fi = factor[:, 2 * k : 2 * k + 1], factor[:, 2 * k + 1 : 2 * k + 2]
            mr = factor[:, MIXED + 2 * k : MIXED + 2 * k + 1]
            mi = signed[:, MIXED + 2 * k + 1 : MIXED + 2 * k + 2]
            re, im = values[source, :, :waves], values[source, :, waves : 2 * waves]
            real += fr * re - fi * im
            imag += fr * im + fi * re
            mixed += mr * values[source, :, 2 * waves :] + mi * turned[source]
        out[t] = jnp.concatenate([real, imag, mixed], axis=1).astype(BF16)

    def result(step):
        part = pl.ds(8 * step, 8)
        return pltpu.make_async_copy(out.at[part], out_at.at[part], sems.at[step])

    for step in range(group // 8):
        for t in range(8):
            target(8 * step + t)
        result(step).start()
    for step in range(group // 8):
        result(step).wait()


def gate_kernel(arrived, out):
    pass


def gate(arrived, cost):
    return pl.pallas_call(
        gate_kernel,
        out_shape=jax.ShapeDtypeStruct(arrived.shape, arrived.dtype),
        in_specs=[ANY],
        out_specs=ANY,
        input_output_aliases={0: 0},
        name="gate",
        **params(cost, 0),
    )(arrived)


def came_relayed(place):
    end = lax.rem(place[0], 4)
    return ((end == 0) | (end == 3)) & (lax.rem(place[1], 2) == 1)


def select_kernel(place, codes, currents, across, beyond, relayed, to_other, to_sibling):
    spot = place[1]
    turned = came_relayed(place)
    for step, out in ((-1, to_other), (1, to_sibling)):
        partner = jnp.where(lax.rem(spot, 2) == 0, spot + step, spot - step)
        code = codes[jnp.clip(partner, 0, codes.shape[0] - 1), CODE]
        same = (code == 3) | (code == 4)
        use_across = (code > 4) == (lax.rem(place[0], 2) == 0)
        for source, wanted in (
            (currents, same),
            (across, jnp.logical_not(same) & use_across),
            (beyond, jnp.logical_not(same | use_across | turned)),
            (relayed, jnp.logical_not(same | use_across) & turned),
        ):

            @pl.when(wanted)
            def _(source=source, out=out):
                out[...] = source[...]


def receive_kernel(incoming, receive, currents, blocks, out):
    group, _, width = incoming.shape
    waves = width // 3
    reals, imags = [], []
    for pair in range(group // 2):
        first = incoming[2 * pair].astype(F32)
        second = incoming[2 * pair + 1].astype(F32)
        mixed = split_rows(first[:, 2 * waves :], second[:, 2 * waves :])
        reals += [first[:, :waves], mixed[0], second[:, :waves]]
        imags += [first[:, waves : 2 * waves], mixed[1], second[:, waves : 2 * waves]]
    left_re = jnp.concatenate(reals, axis=0).T.astype(BF16)
    left_im = jnp.concatenate(imags, axis=0).T.astype(BF16)
    real, imag = product(left_re, left_im, receive)
    own_re, own_im = product(currents[0], currents[1], blocks.at[0, 0])
    out[0] = own_re + real
    out[1] = own_im + imag


def near_kernel(place, near_list, partial, across, beyond, relayed, other, sibling, blocks, out_at, chosen, out, out_sems):
    code = near_list[0, 0]
    straight = (code == 1) | (code == 6)
    use_across = (code > 4) == (lax.rem(place[0], 2) == 0)
    onward = (code == 2) | (code == 4) | (code == 7)
    turned = came_relayed(place)
    use_sibling = onward == (lax.rem(place[1], 2) == 0)
    for source, wanted in (
        (across, straight & use_across),
        (beyond, straight & jnp.logical_not(use_across | turned)),
        (relayed, straight & jnp.logical_not(use_across) & turned),
        (sibling, jnp.logical_not(straight) & use_sibling),
        (other, jnp.logical_not(straight) & jnp.logical_not(use_sibling)),
    ):

        @pl.when(wanted)
        def _(source=source):
            chosen[...] = source[...]

    half = chosen.shape[1] // 2

    def result(part, step):
        rows = pl.ds(step * half, half)
        return pltpu.make_async_copy(out.at[part, rows], out_at.at[0, part, rows], out_sems.at[2 * part + step])

    for step in range(2):
        rows = pl.ds(step * half, half)
        real, imag = product(chosen[0, rows], chosen[1, rows], blocks.at[0, 1])
        for part, value in enumerate((real, imag)):
            out[part, rows] = (partial[part, rows] + value).astype(BF16)
            result(part, step).start()
    for step in range(2):
        for part in range(2):
            result(part, step).wait()


def per_device(
    currents, near_blocks, near_list, radiate, receive, far_list, far_count, owner, translation
):
    local = currents[0]
    _, waves, unknowns = local.shape
    angles = radiate.shape[-1]
    slabs, group = lax.axis_size("blk"), lax.axis_size("bulk")
    row = 4
    place = jnp.stack([lax.axis_index("blk"), lax.axis_index("bulk")]).astype(I32)
    inner = [(i, i ^ 1) for i in range(slabs)]
    outer = [(i, j) for m in range(1, slabs - 1, 2) for i, j in ((m, m + 1), (m + 1, m))]
    side_inner = [(i, i ^ 1) for i in range(group)]
    side_outer = [(i, j) for m in range(1, group - 1, 2) for i, j in ((m, m + 1), (m + 1, m))]
    chunk = 3 * waves
    payload = pl.pallas_call(
        radiate_kernel,
        out_shape=jax.ShapeDtypeStruct((group, 8, chunk + 128), BF16),
        in_specs=[ANY] * 7,
        out_specs=HBM,
        scratch_shapes=[
            pltpu.SMEM(far_list.shape, I32),
            pltpu.SMEM(far_count.shape, I32),
            pltpu.SMEM(near_list.shape, I32),
            pltpu.SMEM(owner.shape, I32),
            pltpu.VMEM(local.shape, BF16),
            pltpu.VMEM(radiate.shape[1:], BF16),
            pltpu.VMEM(translation.shape[1:], F32),
            pltpu.VMEM((128, angles), F32),
            pltpu.VMEM((group, 8, chunk + 128), BF16),
            pltpu.SemaphoreType.DMA((9,)),
            pltpu.SemaphoreType.DMA((4,)),
        ],
        name="radiate",
        **params(8 * waves * unknowns * angles, 2 << 20, 60 << 20),
    )(far_list, far_count, near_list, owner, local, radiate[0], translation[0])
    spread = lax.all_to_all(payload, "bulk", 0, 0, tiled=True)
    axes = ("blk", "bulk")
    direct, aside, onward = [], [], []
    for i, j in outer:
        for spot in range(group):
            if min(i, j) % row == row - 1 and spot % 2:
                turn = i - i % row if i < j else i + row - 1
                aside.append((i * group + spot, turn * group + spot))
                onward.append((turn * group + spot, j * group + spot))
            else:
                direct.append((i * group + spot, j * group + spot))
    relayed = gate(lax.ppermute(local, axes, aside), 3_000_000_000)
    beyond = lax.ppermute(local, axes, direct), lax.ppermute(relayed, axes, onward)
    across = lax.ppermute(local, "blk", inner)
    translated, codes = pl.pallas_call(
        translate_kernel,
        out_shape=(
            jax.ShapeDtypeStruct((group, 8, chunk), BF16),
            jax.ShapeDtypeStruct((group, 128), I32),
        ),
        in_specs=[VMEM],
        out_specs=(HBM, VMEM),
        scratch_shapes=[
            pltpu.VMEM((group, 8, chunk), BF16),
            pltpu.VMEM((group, 8, chunk), F32),
            pltpu.VMEM((group, 8, waves), F32),
            pltpu.VMEM((group, 128), I32),
            pltpu.SMEM((group, 128), I32),
            pltpu.SemaphoreType.DMA,
            pltpu.SemaphoreType.DMA((group // 8,)),
        ],
        name="translate",
        **params(40 << 20, 1 << 20),
    )(spread)
    incoming = lax.all_to_all(translated, "bulk", 0, 0, tiled=True)
    to_other, to_sibling = pl.pallas_call(
        select_kernel,
        out_shape=(jax.ShapeDtypeStruct(local.shape, BF16),) * 2,
        in_specs=[SMEM] * 2 + [VMEM] * 4,
        out_specs=(VMEM, VMEM),
        name="select",
        **params(0, 2 << 20),
    )(place, codes, local, across, *beyond)
    other = lax.ppermute(to_other, "bulk", side_outer)
    sibling = lax.ppermute(to_sibling, "bulk", side_inner)
    partial = pl.pallas_call(
        receive_kernel,
        out_shape=jax.ShapeDtypeStruct((2, waves, unknowns), F32),
        in_specs=[VMEM] * 4,
        out_specs=VMEM,
        name="receive",
        **params(8 * waves * unknowns * angles, 3 << 20),
    )(incoming, receive[0], local, near_blocks)
    return pl.pallas_call(
        near_kernel,
        out_shape=jax.ShapeDtypeStruct((1, *local.shape), BF16),
        in_specs=[SMEM] * 2 + [VMEM] * 7,
        out_specs=HBM,
        scratch_shapes=[
            pltpu.VMEM(local.shape, BF16),
            pltpu.VMEM(local.shape, BF16),
            pltpu.SemaphoreType.DMA((4,)),
        ],
        name="near",
        **params(8 * waves * unknowns * unknowns, 5 << 20),
    )(place, near_list, partial, across, *beyond, other, sibling, near_blocks)


def solution(mesh):
    boxes = ("blk", "bulk")
    return jax.shard_map(
        per_device,
        mesh=mesh,
        in_specs=(
            P(boxes, None, None, None),
            P(boxes, None, None, None, None),
            P(boxes, None),
            P(boxes, None, None, None),
            P(boxes, None, None, None),
            P(boxes, None),
            P(boxes),
            P(),
            P(boxes, None, None, None),
        ),
        out_specs=P(boxes, None, None, None),
        check_vma=False,
    )
```

```python
import jax
import jax.numpy as jnp
from jax import lax
from jax.experimental import pallas as pl
from jax.experimental.pallas import tpu as pltpu
from jax.sharding import PartitionSpec as P

F32, BF16, I32 = jnp.float32, jnp.bfloat16, jnp.int32
VMEM = pl.BlockSpec(memory_space=pltpu.VMEM)
SMEM = pl.BlockSpec(memory_space=pltpu.SMEM)
ANY = pl.BlockSpec(memory_space=pl.ANY)
HBM = pl.BlockSpec(memory_space=pltpu.HBM)
LOW, MIXED, SOURCE, CODE = 16, 32, 64, 72


def dot(left, right):
    return jnp.dot(left, right, preferred_element_type=F32)


def product(left_re, left_im, right):
    return (
        dot(left_re, right[0]) - dot(left_im, right[1]),
        dot(left_re, right[1]) + dot(left_im, right[0]),
    )


def params(flops, moved, limit=40 << 20):
    return dict(
        compiler_params=pltpu.CompilerParams(vmem_limit_bytes=limit),
        cost_estimate=pl.CostEstimate(flops=flops, bytes_accessed=moved, transcendentals=0),
    )


def split_rows(first, second):
    top = lax.broadcasted_iota(I32, first.shape, 0) < 4
    return (
        jnp.where(top, first, pltpu.roll(second, 4, 0)),
        jnp.where(top, pltpu.roll(first, 4, 0), second),
    )


def radiate_kernel(
    far_list_at, far_count_at, near_list_at, owner_at, currents_at, radiate_at, translation_at, out_at,
    far_list, far_count, near_list, owner, currents, radiate, translation, table, out, sems, out_sems,
):
    small = (
        (far_list_at, far_list),
        (far_count_at, far_count),
        (near_list_at, near_list),
        (owner_at, owner),
        (translation_at, translation),
    )
    large = [(currents_at.at[p], currents.at[p]) for p in range(2)]
    large += [(radiate_at.at[p], radiate.at[p]) for p in range(2)]
    copies = [
        pltpu.make_async_copy(source, target, sems.at[n])
        for n, (source, target) in enumerate((*small, *large))
    ]
    for copy in copies:
        copy.start()
    group, _, width = out.shape
    angles = table.shape[1]
    far = translation.shape[0]
    table[...] = jnp.zeros_like(table)
    for copy in copies[: len(small)]:
        copy.wait()
    for k in range(far):
        factor = jnp.where(k < far_count[0], translation[k], 0.0)
        high = factor.astype(BF16).astype(F32)
        for base in (0, MIXED):
            table[base + 2 * k : base + 2 * k + 2, :] = high
            table[base + LOW + 2 * k : base + LOW + 2 * k + 2, :] = factor - high
        source = lax.rem(owner[far_list[0, k]], group).astype(F32)
        table[SOURCE + k : SOURCE + k + 1, :] = jnp.full((1, angles), source, F32)
    table[CODE : CODE + 1, :] = jnp.full((1, angles), near_list[0, 0].astype(F32), F32)
    for copy in copies[len(small) :]:
        copy.wait()
    waves = currents.shape[1]

    def turned(part, side):
        return lax.dot_general(radiate[part], currents[side], (((0,), (1,)), ((), ())), preferred_element_type=F32)

    real = turned(0, 0) - turned(1, 1)
    imag = turned(1, 0) + turned(0, 1)
    tiles = angles // 8
    real = real.reshape(tiles, 8, waves)
    imag = imag.reshape(tiles, 8, waves)
    factors = table[...].T.reshape(tiles, 8, table.shape[0])
    lane = lax.broadcasted_iota(I32, factors.shape[1:], 1)
    in_mixed = (lane >= MIXED) & (lane < SOURCE)
    def result(step):
        part = pl.ds(group // 4 * step, group // 4)
        return pltpu.make_async_copy(out.at[part], out_at.at[part], out_sems.at[step])

    for pair in range(group // 2):
        a, b, c = 3 * pair, 3 * pair + 1, 3 * pair + 2
        mixed = split_rows(real[b], imag[b])
        mixed_factors = split_rows(factors[b], factors[b])
        for side, tile in ((0, a), (1, c)):
            beside = jnp.where(in_mixed, mixed_factors[side], factors[tile])
            whole = jnp.concatenate([real[tile], imag[tile], mixed[side], beside], axis=1)
            out[2 * pair + side] = whole.astype(BF16)
        if pair % (group // 8) == group // 8 - 1:
            result(pair // (group // 8)).start()
    for step in range(4):
        result(step).wait()


def translate_kernel(chunks_at, out, codes, chunks, values, turned, numbers, table, sem, sems):
    group, _, width = out.shape
    waves = width // 3
    arrivals = []
    for step in range(group // 8):
        part = pl.ds(8 * step, 8)
        arrivals.append(pltpu.make_async_copy(chunks_at.at[part], chunks.at[part], sems.at[step]))
        arrivals[-1].start()
    for step, arrival in enumerate(arrivals):
        arrival.wait()
        for t in range(8 * step, 8 * step + 8):
            numbers[t : t + 1, :] = chunks[t, :, width:].astype(F32)[0:1, :].astype(I32)
            values[t] = chunks[t, :, :width].astype(F32)
            turned[t] = pltpu.roll(values[t, :, 2 * waves :], 4, 0)
    copy = pltpu.make_async_copy(numbers, table, sem)
    copy.start()
    codes[...] = numbers[...]
    copy.wait()
    sign = jnp.where(lax.broadcasted_iota(I32, (8, 128), 0) < 4, -1.0, 1.0)

    def target(t):
        split = chunks[t, :, width:].astype(F32)
        factor = split + pltpu.roll(split, 128 - LOW, 1)
        signed = factor * sign
        real = jnp.zeros((8, waves), F32)
        imag, mixed = real, real
        for k in range(6):
            source = table[t, SOURCE + k]
            fr, fi = factor[:, 2 * k : 2 * k + 1], factor[:, 2 * k + 1 : 2 * k + 2]
            mr = factor[:, MIXED + 2 * k : MIXED + 2 * k + 1]
            mi = signed[:, MIXED + 2 * k + 1 : MIXED + 2 * k + 2]
            re, im = values[source, :, :waves], values[source, :, waves : 2 * waves]
            real += fr * re - fi * im
            imag += fr * im + fi * re
            mixed += mr * values[source, :, 2 * waves :] + mi * turned[source]
        out[t] = jnp.concatenate([real, imag, mixed], axis=1).astype(BF16)

    for step in range(group // 8):
        for t in range(8):
            target(8 * step + t)


def gate_kernel(arrived, out):
    pass


def gate(arrived, cost):
    return pl.pallas_call(
        gate_kernel,
        out_shape=jax.ShapeDtypeStruct(arrived.shape, arrived.dtype),
        in_specs=[ANY],
        out_specs=ANY,
        input_output_aliases={0: 0},
        name="gate",
        **params(cost, 0),
    )(arrived)


def came_relayed(place):
    end = lax.rem(place[0], 4)
    return ((end == 0) | (end == 3)) & (lax.rem(place[1], 2) == 1)


def select_kernel(place, codes, currents, across, beyond, relayed, to_other, to_sibling):
    spot = place[1]
    turned = came_relayed(place)
    for step, out in ((-1, to_other), (1, to_sibling)):
        partner = jnp.where(lax.rem(spot, 2) == 0, spot + step, spot - step)
        code = codes[jnp.clip(partner, 0, codes.shape[0] - 1), CODE]
        same = (code == 3) | (code == 4)
        use_across = (code > 4) == (lax.rem(place[0], 2) == 0)
        for source, wanted in (
            (currents, same),
            (across, jnp.logical_not(same) & use_across),
            (beyond, jnp.logical_not(same | use_across | turned)),
            (relayed, jnp.logical_not(same | use_across) & turned),
        ):

            @pl.when(wanted)
            def _(source=source, out=out):
                out[...] = source[...]


def receive_kernel(place, near_list, incoming, receive, currents, blocks, across, beyond, relayed, out, mine):
    use_across = (near_list[0, 0] > 4) == (lax.rem(place[0], 2) == 0)
    turned = came_relayed(place)
    for source, wanted in (
        (across, use_across),
        (beyond, jnp.logical_not(use_across | turned)),
        (relayed, jnp.logical_not(use_across) & turned),
    ):

        @pl.when(wanted)
        def _(source=source):
            mine[...] = source[...]

    group, _, width = incoming.shape
    waves = width // 3
    reals, imags = [], []
    for pair in range(group // 2):
        first = incoming[2 * pair].astype(F32)
        second = incoming[2 * pair + 1].astype(F32)
        mixed = split_rows(first[:, 2 * waves :], second[:, 2 * waves :])
        reals += [first[:, :waves], mixed[0], second[:, :waves]]
        imags += [first[:, waves : 2 * waves], mixed[1], second[:, waves : 2 * waves]]
    left_re = jnp.concatenate(reals, axis=0).T.astype(BF16)
    left_im = jnp.concatenate(imags, axis=0).T.astype(BF16)
    real, imag = product(left_re, left_im, receive)
    own_re, own_im = product(currents[0], currents[1], blocks.at[0, 0])
    out[0] = own_re + real
    out[1] = own_im + imag


def near_kernel(place, near_list, partial, mine, other, sibling, blocks, out_at, chosen, out, out_sems):
    code = near_list[0, 0]
    straight = (code == 1) | (code == 6)
    onward = (code == 2) | (code == 4) | (code == 7)
    use_sibling = onward == (lax.rem(place[1], 2) == 0)
    for source, wanted in (
        (mine, straight),
        (sibling, jnp.logical_not(straight) & use_sibling),
        (other, jnp.logical_not(straight) & jnp.logical_not(use_sibling)),
    ):

        @pl.when(wanted)
        def _(source=source):
            chosen[...] = source[...]

    half = chosen.shape[1] // 2

    def result(part, step):
        rows = pl.ds(step * half, half)
        return pltpu.make_async_copy(out.at[part, rows], out_at.at[0, part, rows], out_sems.at[2 * part + step])

    for step in range(2):
        rows = pl.ds(step * half, half)
        real, imag = product(chosen[0, rows], chosen[1, rows], blocks.at[0, 1])
        for part, value in enumerate((real, imag)):
            out[part, rows] = (partial[part, rows] + value).astype(BF16)
            result(part, step).start()
    for step in range(2):
        for part in range(2):
            result(part, step).wait()


def per_device(
    currents, near_blocks, near_list, radiate, receive, far_list, far_count, owner, translation
):
    local = currents[0]
    _, waves, unknowns = local.shape
    angles = radiate.shape[-1]
    slabs, group = lax.axis_size("blk"), lax.axis_size("bulk")
    row = 4
    place = jnp.stack([lax.axis_index("blk"), lax.axis_index("bulk")]).astype(I32)
    inner = [(i, i ^ 1) for i in range(slabs)]
    outer = [(i, j) for m in range(1, slabs - 1, 2) for i, j in ((m, m + 1), (m + 1, m))]
    side_inner = [(i, i ^ 1) for i in range(group)]
    side_outer = [(i, j) for m in range(1, group - 1, 2) for i, j in ((m, m + 1), (m + 1, m))]
    chunk = 3 * waves
    payload = pl.pallas_call(
        radiate_kernel,
        out_shape=jax.ShapeDtypeStruct((group, 8, chunk + 128), BF16),
        in_specs=[ANY] * 7,
        out_specs=HBM,
        scratch_shapes=[
            pltpu.SMEM(far_list.shape, I32),
            pltpu.SMEM(far_count.shape, I32),
            pltpu.SMEM(near_list.shape, I32),
            pltpu.SMEM(owner.shape, I32),
            pltpu.VMEM(local.shape, BF16),
            pltpu.VMEM(radiate.shape[1:], BF16),
            pltpu.VMEM(translation.shape[1:], F32),
            pltpu.VMEM((128, angles), F32),
            pltpu.VMEM((group, 8, chunk + 128), BF16),
            pltpu.SemaphoreType.DMA((9,)),
            pltpu.SemaphoreType.DMA((4,)),
        ],
        name="radiate",
        **params(8 * waves * unknowns * angles, 2 << 20, 60 << 20),
    )(far_list, far_count, near_list, owner, local, radiate[0], translation[0])
    spread = lax.all_to_all(payload, "bulk", 0, 0, tiled=True)
    axes = ("blk", "bulk")
    direct, aside, onward = [], [], []
    for i, j in outer:
        for spot in range(group):
            if min(i, j) % row == row - 1 and spot % 2:
                turn = i - i % row if i < j else i + row - 1
                aside.append((i * group + spot, turn * group + spot))
                onward.append((turn * group + spot, j * group + spot))
            else:
                direct.append((i * group + spot, j * group + spot))
    relayed = gate(lax.ppermute(local, axes, aside), 3_000_000_000)
    beyond = lax.ppermute(local, axes, direct), lax.ppermute(relayed, axes, onward)
    across = lax.ppermute(local, "blk", inner)
    translated, codes = pl.pallas_call(
        translate_kernel,
        out_shape=(
            jax.ShapeDtypeStruct((group, 8, chunk), BF16),
            jax.ShapeDtypeStruct((group, 128), I32),
        ),
        in_specs=[ANY],
        out_specs=(VMEM, VMEM),
        scratch_shapes=[
            pltpu.VMEM((group, 8, chunk + 128), BF16),
            pltpu.VMEM((group, 8, chunk), F32),
            pltpu.VMEM((group, 8, waves), F32),
            pltpu.VMEM((group, 128), I32),
            pltpu.SMEM((group, 128), I32),
            pltpu.SemaphoreType.DMA,
            pltpu.SemaphoreType.DMA((group // 8,)),
        ],
        name="translate",
        **params(40 << 20, 1 << 20),
    )(spread)
    incoming = lax.all_to_all(translated, "bulk", 0, 0, tiled=True)
    to_other, to_sibling = pl.pallas_call(
        select_kernel,
        out_shape=(jax.ShapeDtypeStruct(local.shape, BF16),) * 2,
        in_specs=[SMEM] * 2 + [VMEM] * 4,
        out_specs=(VMEM, VMEM),
        name="select",
        **params(0, 2 << 20),
    )(place, codes, local, across, *beyond)
    other = lax.ppermute(to_other, "bulk", side_outer)
    sibling = lax.ppermute(to_sibling, "bulk", side_inner)
    partial, mine = pl.pallas_call(
        receive_kernel,
        out_shape=(
            jax.ShapeDtypeStruct((2, waves, unknowns), F32),
            jax.ShapeDtypeStruct(local.shape, BF16),
        ),
        in_specs=[SMEM] * 2 + [VMEM] * 7,
        out_specs=(VMEM, VMEM),
        name="receive",
        **params(8 * waves * unknowns * angles, 3 << 20),
    )(place, near_list, incoming, receive[0], local, near_blocks, across, *beyond)
    return pl.pallas_call(
        near_kernel,
        out_shape=jax.ShapeDtypeStruct((1, *local.shape), BF16),
        in_specs=[SMEM] * 2 + [VMEM] * 5,
        out_specs=HBM,
        scratch_shapes=[
            pltpu.VMEM(local.shape, BF16),
            pltpu.VMEM(local.shape, BF16),
            pltpu.SemaphoreType.DMA((4,)),
        ],
        name="near",
        **params(8 * waves * unknowns * unknowns, 5 << 20),
    )(place, near_list, partial, mine, other, sibling, near_blocks)


def solution(mesh):
    boxes = ("blk", "bulk")
    return jax.shard_map(
        per_device,
        mesh=mesh,
        in_specs=(
            P(boxes, None, None, None),
            P(boxes, None, None, None, None),
            P(boxes, None),
            P(boxes, None, None, None),
            P(boxes, None, None, None),
            P(boxes, None),
            P(boxes),
            P(),
            P(boxes, None, None, None),
        ),
        out_specs=P(boxes, None, None, None),
        check_vma=False,
    )
```

```python
import jax
import jax.numpy as jnp
from jax import lax
from jax.experimental import pallas as pl
from jax.experimental.pallas import tpu as pltpu
from jax.sharding import PartitionSpec as P

F32, BF16, I32 = jnp.float32, jnp.bfloat16, jnp.int32
VMEM = pl.BlockSpec(memory_space=pltpu.VMEM)
SMEM = pl.BlockSpec(memory_space=pltpu.SMEM)
ANY = pl.BlockSpec(memory_space=pl.ANY)
HBM = pl.BlockSpec(memory_space=pltpu.HBM)
LOW, MIXED, SOURCE, CODE = 16, 32, 64, 72


def dot(left, right):
    return jnp.dot(left, right, preferred_element_type=F32)


def product(left_re, left_im, right):
    return (
        dot(left_re, right[0]) - dot(left_im, right[1]),
        dot(left_re, right[1]) + dot(left_im, right[0]),
    )


def params(flops, moved, limit=40 << 20):
    return dict(
        compiler_params=pltpu.CompilerParams(vmem_limit_bytes=limit),
        cost_estimate=pl.CostEstimate(flops=flops, bytes_accessed=moved, transcendentals=0),
    )


def split_rows(first, second):
    top = lax.broadcasted_iota(I32, first.shape, 0) < 4
    return (
        jnp.where(top, first, pltpu.roll(second, 4, 0)),
        jnp.where(top, pltpu.roll(first, 4, 0), second),
    )


def radiate_kernel(
    far_list_at, far_count_at, near_list_at, owner_at, currents_at, radiate_at, translation_at, out_at,
    far_list, far_count, near_list, owner, currents, radiate, translation, table, out, sems, out_sems,
):
    small = (
        (far_list_at, far_list),
        (far_count_at, far_count),
        (near_list_at, near_list),
        (owner_at, owner),
        (translation_at, translation),
    )
    large = [(currents_at.at[p], currents.at[p]) for p in range(2)]
    large += [(radiate_at.at[p], radiate.at[p]) for p in range(2)]
    copies = [
        pltpu.make_async_copy(source, target, sems.at[n])
        for n, (source, target) in enumerate((*small, *large))
    ]
    for copy in copies:
        copy.start()
    group, _, width = out.shape
    angles = table.shape[1]
    far = translation.shape[0]
    table[...] = jnp.zeros_like(table)
    for copy in copies[: len(small)]:
        copy.wait()
    for k in range(far):
        factor = jnp.where(k < far_count[0], translation[k], 0.0)
        high = factor.astype(BF16).astype(F32)
        for base in (0, MIXED):
            table[base + 2 * k : base + 2 * k + 2, :] = high
            table[base + LOW + 2 * k : base + LOW + 2 * k + 2, :] = factor - high
        source = lax.rem(owner[far_list[0, k]], group).astype(F32)
        table[SOURCE + k : SOURCE + k + 1, :] = jnp.full((1, angles), source, F32)
    table[CODE : CODE + 1, :] = jnp.full((1, angles), near_list[0, 0].astype(F32), F32)
    tiles = angles // 8
    factors = table[...].T.reshape(tiles, 8, table.shape[0])
    waves = currents.shape[1]

    def turned(part, side):
        return lax.dot_general(radiate[part], currents[side], (((0,), (1,)), ((), ())), preferred_element_type=F32)

    re_waves, im_waves, re_map, im_map = copies[len(small) :]
    re_waves.wait()
    re_map.wait()
    real = turned(0, 0)
    im_waves.wait()
    imag = turned(0, 1)
    im_map.wait()
    real = (real - turned(1, 1)).reshape(tiles, 8, waves)
    imag = (imag + turned(1, 0)).reshape(tiles, 8, waves)
    lane = lax.broadcasted_iota(I32, factors.shape[1:], 1)
    in_mixed = (lane >= MIXED) & (lane < SOURCE)
    def result(step):
        part = pl.ds(group // 4 * step, group // 4)
        return pltpu.make_async_copy(out.at[part], out_at.at[part], out_sems.at[step])

    for pair in range(group // 2):
        a, b, c = 3 * pair, 3 * pair + 1, 3 * pair + 2
        mixed = split_rows(real[b], imag[b])
        mixed_factors = split_rows(factors[b], factors[b])
        for side, tile in ((0, a), (1, c)):
            beside = jnp.where(in_mixed, mixed_factors[side], factors[tile])
            whole = jnp.concatenate([real[tile], imag[tile], mixed[side], beside], axis=1)
            out[2 * pair + side] = whole.astype(BF16)
        if pair % (group // 8) == group // 8 - 1:
            result(pair // (group // 8)).start()
    for step in range(4):
        result(step).wait()


def translate_kernel(chunks_at, out, codes, chunks, values, turned, numbers, table, sem, sems):
    group, _, width = out.shape
    waves = width // 3
    arrivals = []
    for step in range(group // 8):
        part = pl.ds(8 * step, 8)
        arrivals.append(pltpu.make_async_copy(chunks_at.at[part], chunks.at[part], sems.at[step]))
        arrivals[-1].start()
    for step, arrival in enumerate(arrivals):
        arrival.wait()
        for t in range(8 * step, 8 * step + 8):
            numbers[t : t + 1, :] = chunks[t, :, width:].astype(F32)[0:1, :].astype(I32)
            values[t] = chunks[t, :, :width].astype(F32)
            turned[t] = pltpu.roll(values[t, :, 2 * waves :], 4, 0)
    copy = pltpu.make_async_copy(numbers, table, sem)
    copy.start()
    codes[...] = numbers[...]
    copy.wait()
    sign = jnp.where(lax.broadcasted_iota(I32, (8, 128), 0) < 4, -1.0, 1.0)

    def target(t):
        split = chunks[t, :, width:].astype(F32)
        factor = split + pltpu.roll(split, 128 - LOW, 1)
        signed = factor * sign
        real = jnp.zeros((8, waves), F32)
        imag, mixed = real, real
        for k in range(6):
            source = table[t, SOURCE + k]
            fr, fi = factor[:, 2 * k : 2 * k + 1], factor[:, 2 * k + 1 : 2 * k + 2]
            mr = factor[:, MIXED + 2 * k : MIXED + 2 * k + 1]
            mi = signed[:, MIXED + 2 * k + 1 : MIXED + 2 * k + 2]
            re, im = values[source, :, :waves], values[source, :, waves : 2 * waves]
            real += fr * re - fi * im
            imag += fr * im + fi * re
            mixed += mr * values[source, :, 2 * waves :] + mi * turned[source]
        out[t] = jnp.concatenate([real, imag, mixed], axis=1).astype(BF16)

    for step in range(group // 8):
        for t in range(8):
            target(8 * step + t)


def gate_kernel(arrived, out):
    pass


def gate(arrived, cost):
    return pl.pallas_call(
        gate_kernel,
        out_shape=jax.ShapeDtypeStruct(arrived.shape, arrived.dtype),
        in_specs=[ANY],
        out_specs=ANY,
        input_output_aliases={0: 0},
        name="gate",
        **params(cost, 0),
    )(arrived)


def came_relayed(place):
    end = lax.rem(place[0], 4)
    return ((end == 0) | (end == 3)) & (lax.rem(place[1], 2) == 1)


def select_kernel(place, codes, currents, across, beyond, relayed, to_other, to_sibling):
    spot = place[1]
    turned = came_relayed(place)
    for step, out in ((-1, to_other), (1, to_sibling)):
        partner = jnp.where(lax.rem(spot, 2) == 0, spot + step, spot - step)
        code = codes[jnp.clip(partner, 0, codes.shape[0] - 1), CODE]
        same = (code == 3) | (code == 4)
        use_across = (code > 4) == (lax.rem(place[0], 2) == 0)
        for source, wanted in (
            (currents, same),
            (across, jnp.logical_not(same) & use_across),
            (beyond, jnp.logical_not(same | use_across | turned)),
            (relayed, jnp.logical_not(same | use_across) & turned),
        ):

            @pl.when(wanted)
            def _(source=source, out=out):
                out[...] = source[...]


def receive_kernel(place, near_list, incoming, receive, currents, blocks, across, beyond, relayed, out, mine):
    use_across = (near_list[0, 0] > 4) == (lax.rem(place[0], 2) == 0)
    turned = came_relayed(place)
    for source, wanted in (
        (across, use_across),
        (beyond, jnp.logical_not(use_across | turned)),
        (relayed, jnp.logical_not(use_across) & turned),
    ):

        @pl.when(wanted)
        def _(source=source):
            mine[...] = source[...]

    group, _, width = incoming.shape
    waves = width // 3
    reals, imags = [], []
    for pair in range(group // 2):
        first = incoming[2 * pair].astype(F32)
        second = incoming[2 * pair + 1].astype(F32)
        mixed = split_rows(first[:, 2 * waves :], second[:, 2 * waves :])
        reals += [first[:, :waves], mixed[0], second[:, :waves]]
        imags += [first[:, waves : 2 * waves], mixed[1], second[:, waves : 2 * waves]]
    left_re = jnp.concatenate(reals, axis=0).T.astype(BF16)
    left_im = jnp.concatenate(imags, axis=0).T.astype(BF16)
    real, imag = product(left_re, left_im, receive)
    own_re, own_im = product(currents[0], currents[1], blocks.at[0, 0])
    out[0] = own_re + real
    out[1] = own_im + imag


def near_kernel(place, near_list, partial, mine, other, sibling, blocks, out_at, chosen, out, out_sems):
    code = near_list[0, 0]
    straight = (code == 1) | (code == 6)
    onward = (code == 2) | (code == 4) | (code == 7)
    use_sibling = onward == (lax.rem(place[1], 2) == 0)
    for source, wanted in (
        (mine, straight),
        (sibling, jnp.logical_not(straight) & use_sibling),
        (other, jnp.logical_not(straight) & jnp.logical_not(use_sibling)),
    ):

        @pl.when(wanted)
        def _(source=source):
            chosen[...] = source[...]

    half = chosen.shape[1] // 2

    def result(part, step):
        rows = pl.ds(step * half, half)
        return pltpu.make_async_copy(out.at[part, rows], out_at.at[0, part, rows], out_sems.at[2 * part + step])

    for step in range(2):
        rows = pl.ds(step * half, half)
        real, imag = product(chosen[0, rows], chosen[1, rows], blocks.at[0, 1])
        for part, value in enumerate((real, imag)):
            out[part, rows] = (partial[part, rows] + value).astype(BF16)
            result(part, step).start()
    for step in range(2):
        for part in range(2):
            result(part, step).wait()


def per_device(
    currents, near_blocks, near_list, radiate, receive, far_list, far_count, owner, translation
):
    local = currents[0]
    _, waves, unknowns = local.shape
    angles = radiate.shape[-1]
    slabs, group = lax.axis_size("blk"), lax.axis_size("bulk")
    row = 4
    place = jnp.stack([lax.axis_index("blk"), lax.axis_index("bulk")]).astype(I32)
    inner = [(i, i ^ 1) for i in range(slabs)]
    outer = [(i, j) for m in range(1, slabs - 1, 2) for i, j in ((m, m + 1), (m + 1, m))]
    side_inner = [(i, i ^ 1) for i in range(group)]
    side_outer = [(i, j) for m in range(1, group - 1, 2) for i, j in ((m, m + 1), (m + 1, m))]
    chunk = 3 * waves
    payload = pl.pallas_call(
        radiate_kernel,
        out_shape=jax.ShapeDtypeStruct((group, 8, chunk + 128), BF16),
        in_specs=[ANY] * 7,
        out_specs=HBM,
        scratch_shapes=[
            pltpu.SMEM(far_list.shape, I32),
            pltpu.SMEM(far_count.shape, I32),
            pltpu.SMEM(near_list.shape, I32),
            pltpu.SMEM(owner.shape, I32),
            pltpu.VMEM(local.shape, BF16),
            pltpu.VMEM(radiate.shape[1:], BF16),
            pltpu.VMEM(translation.shape[1:], F32),
            pltpu.VMEM((128, angles), F32),
            pltpu.VMEM((group, 8, chunk + 128), BF16),
            pltpu.SemaphoreType.DMA((9,)),
            pltpu.SemaphoreType.DMA((4,)),
        ],
        name="radiate",
        **params(8 * waves * unknowns * angles, 2 << 20, 60 << 20),
    )(far_list, far_count, near_list, owner, local, radiate[0], translation[0])
    spread = lax.all_to_all(payload, "bulk", 0, 0, tiled=True)
    axes = ("blk", "bulk")
    direct, aside, onward = [], [], []
    for i, j in outer:
        for spot in range(group):
            if min(i, j) % row == row - 1 and spot % 2:
                turn = i - i % row if i < j else i + row - 1
                aside.append((i * group + spot, turn * group + spot))
                onward.append((turn * group + spot, j * group + spot))
            else:
                direct.append((i * group + spot, j * group + spot))
    relayed = gate(lax.ppermute(local, axes, aside), 3_000_000_000)
    beyond = lax.ppermute(local, axes, direct), lax.ppermute(relayed, axes, onward)
    across = lax.ppermute(local, "blk", inner)
    translated, codes = pl.pallas_call(
        translate_kernel,
        out_shape=(
            jax.ShapeDtypeStruct((group, 8, chunk), BF16),
            jax.ShapeDtypeStruct((group, 128), I32),
        ),
        in_specs=[ANY],
        out_specs=(VMEM, VMEM),
        scratch_shapes=[
            pltpu.VMEM((group, 8, chunk + 128), BF16),
            pltpu.VMEM((group, 8, chunk), F32),
            pltpu.VMEM((group, 8, waves), F32),
            pltpu.VMEM((group, 128), I32),
            pltpu.SMEM((group, 128), I32),
            pltpu.SemaphoreType.DMA,
            pltpu.SemaphoreType.DMA((group // 8,)),
        ],
        name="translate",
        **params(40 << 20, 1 << 20),
    )(spread)
    incoming = lax.all_to_all(translated, "bulk", 0, 0, tiled=True)
    to_other, to_sibling = pl.pallas_call(
        select_kernel,
        out_shape=(jax.ShapeDtypeStruct(local.shape, BF16),) * 2,
        in_specs=[SMEM] * 2 + [VMEM] * 4,
        out_specs=(VMEM, VMEM),
        name="select",
        **params(0, 2 << 20),
    )(place, codes, local, across, *beyond)
    other = lax.ppermute(to_other, "bulk", side_outer)
    sibling = lax.ppermute(to_sibling, "bulk", side_inner)
    partial, mine = pl.pallas_call(
        receive_kernel,
        out_shape=(
            jax.ShapeDtypeStruct((2, waves, unknowns), F32),
            jax.ShapeDtypeStruct(local.shape, BF16),
        ),
        in_specs=[SMEM] * 2 + [VMEM] * 7,
        out_specs=(VMEM, VMEM),
        name="receive",
        **params(8 * waves * unknowns * angles, 3 << 20),
    )(place, near_list, incoming, receive[0], local, near_blocks, across, *beyond)
    return pl.pallas_call(
        near_kernel,
        out_shape=jax.ShapeDtypeStruct((1, *local.shape), BF16),
        in_specs=[SMEM] * 2 + [VMEM] * 5,
        out_specs=HBM,
        scratch_shapes=[
            pltpu.VMEM(local.shape, BF16),
            pltpu.VMEM(local.shape, BF16),
            pltpu.SemaphoreType.DMA((4,)),
        ],
        name="near",
        **params(8 * waves * unknowns * unknowns, 5 << 20),
    )(place, near_list, partial, mine, other, sibling, near_blocks)


def solution(mesh):
    boxes = ("blk", "bulk")
    return jax.shard_map(
        per_device,
        mesh=mesh,
        in_specs=(
            P(boxes, None, None, None),
            P(boxes, None, None, None, None),
            P(boxes, None),
            P(boxes, None, None, None),
            P(boxes, None, None, None),
            P(boxes, None),
            P(boxes),
            P(),
            P(boxes, None, None, None),
        ),
        out_specs=P(boxes, None, None, None),
        check_vma=False,
    )
```
